32 devices in a mesh: groups: 2 (over y), dp: 2 (over core), mp: 8 (over z, x).
Axes of the slice: x: 2, y: 2, z: 4, core: 2. Of those that a mesh axis runs over, the one named last changes fastest.
Arguments:
- tokens: bfloat16 [768, 6144], P(('groups', 'dp'), 'mp'), parts along dimension 0, may hold values from -6 to 6
- row_image: int32 [768], P(('groups', 'dp')), parts along dimension 0, may hold values from 0 to 10, as said below
- norm_gain: bfloat16 [6144], P('mp'), may hold values from 0.099609375 to 1.8984375
- inner_weight: bfloat16 [6144, 24576], P(('dp', 'mp')), may hold values from -0.078125 to 0.078125
- inner_bias: bfloat16 [24576], P(('dp', 'mp')), may hold values from -3 to 3
- outer_weight: bfloat16 [24576, 6144], P(('dp', 'mp')), may hold values from -0.0546875 to 0.0546875
- outer_bias: bfloat16 [6144], P('mp'), may hold values from -3 to 3
Outputs:
- mixed_rows: bfloat16 [768, 6144], P(('groups', 'dp'), 'mp'), parts along dimension 0
- pooled: float32 [20, 6144], P('groups', 'mp'), parts along dimension 0
The draws below stay inside these ranges and needn't reach their ends.
There are 2 independent parts, one for each index of `groups`. The reference program is written for one: setup_inputs(seed, part) draws one part's arguments, and reference() takes and returns one part's arrays. A program takes and returns all parts, laid end to end along the dimension named above; an argument that names none is the same for every part. Nothing has to cross between parts.
Inputs may be any that keep to these rules, and one draw needn't show every extreme that they name: `row_image`: each data shard's 192 rows hold its images one after another from row 0, image k of a shard starting at row k * 32; an image's rows are consecutive and carry its number, all other rows carry 10. Images are numbered upward through shard 0 and then shard 1, every image has 25 to 32 rows, and the last image of each shard has exactly 32. One shard (the loaded one) holds 6 images, with image rows up to row 191; the other holds 4 images, up to row 127. The loaded shard hands its first 32 rows to the other.
All inputs are finite; a program needn't handle non-finite values.
Results may differ from the reference program's by a relative error of at most 0.0043.
Values may be sent and summed in bfloat16 or wider, within the bound.
No kernel may reach another device: no remote copies, remote signals or barrier semaphores. Data moves between devices by JAX's collectives and lax.ppermute only.
A program may use at most 256 MiB of HBM per device.

```python
import jax
import jax.numpy as jnp
from jax import lax

D = 6144
FF = 24576
IMG_SHARD = 5
SEND = 32
ROWS_DEV = 192
ROWS = 384
IMAGES = 10


def draw_row_image(key, part):
    key = jax.random.fold_in(key, 5)
    loaded = jax.random.randint(jax.random.fold_in(key, 11), (), 0, 2)
    lengths = jax.random.randint(jax.random.fold_in(key, 12), (2, IMG_SHARD + 1), SEND - 7, SEND + 1)
    shard_ids = jnp.arange(2, dtype=jnp.int32)[:, None]
    slot_ids = jnp.arange(IMG_SHARD + 1, dtype=jnp.int32)[None, :]
    is_loaded = shard_ids == loaded
    light = jnp.logical_not(is_loaded)
    lengths = jnp.where(is_loaded & ((slot_ids == 0) | (slot_ids == IMG_SHARD)), SEND, lengths)
    lengths = jnp.where(light & (slot_ids == IMG_SHARD - 2), SEND, lengths)
    lengths = jnp.where(light & (slot_ids >= IMG_SHARD - 1), 0, lengths)
    starts = slot_ids * SEND
    first_count = jnp.where(loaded == 0, IMG_SHARD + 1, IMG_SHARD - 1)
    numbers = jnp.where(shard_ids == 0, slot_ids, first_count + slot_ids)
    row_ids = jnp.arange(ROWS_DEV, dtype=jnp.int32)[None, None, :]
    inside = (row_ids >= starts[:, :, None]) & (row_ids < (starts + lengths)[:, :, None])
    image = jnp.sum(jnp.where(inside, numbers[:, :, None] + 1, 0), axis=1) - 1
    image = jnp.where(image < 0, IMAGES, image)
    return image.reshape(ROWS).astype(jnp.int32)


def spiked(values, rng, source, target, blocks, factor):
    def block_of(axis_at):
        return (jnp.arange(values.shape[axis_at]) // (values.shape[axis_at] // blocks)).reshape((-1,) + (1,) * (values.ndim - 1 - axis_at))

    one_side = jax.random.permutation(rng, blocks)[block_of(target)]
    far = (block_of(target) + blocks // 2) % blocks
    return jnp.where((block_of(source) == one_side) | (block_of(source) == far), factor * values, values)


def level_of(rng, extent, split, smallest, top_value):
    factor_of, own = 1.0, jax.random.fold_in(rng, 6)
    for position, blocks in split:
        draws = jnp.exp(jax.random.uniform(jax.random.fold_in(own, position), (blocks,), jnp.float32, smallest / len(split), top_value / len(split)))
        factor_of = factor_of * jnp.repeat(draws, extent[position] // blocks).reshape([-1 if axis == position else 1 for axis in range(len(extent))])
    return factor_of


def noise(key, extent, deviation, limit, shards=(), held_as=jnp.bfloat16):
    result = deviation * jax.random.normal(key, extent, jnp.float32)
    if shards:
        result = result * level_of(key, extent, shards, -0.22, 0.18)
    return jnp.clip(result, -limit, limit).astype(held_as)


def noise_with(rng, shape, width, reach, shards, heavy, kind=jnp.bfloat16):
    entries = width * jax.random.normal(rng, shape, jnp.float32)
    if shards:
        entries = entries * level_of(rng, shape, shards, -0.22, 0.18)
    return jnp.clip(spiked(entries, jax.random.fold_in(rng, 3), *heavy), -reach, reach).astype(kind)


def setup_inputs(seed: int = 0, part: int = 0) -> dict:
    splits = jax.random.split(jax.random.key(seed), 8)
    part_splits = jax.random.split(jax.random.fold_in(splits[7], part), 8)
    return {
        "tokens": noise(part_splits[0], (ROWS, D), 1.0, 6.0, ((0, 2), (1, 8))),
        "row_image": draw_row_image(jax.random.fold_in(jax.random.fold_in(splits[7], part), 71), part),
        "norm_gain": jnp.clip(1.0 + 0.18 * jax.random.normal(splits[2], (D,), jnp.float32), 0.099609375, 1.8984375).astype(jnp.bfloat16),
        "inner_weight": noise(splits[3], (D, FF), D ** -0.5, 0.078125, ((0, 16),)),
        "inner_bias": noise(splits[4], (FF,), 0.5, 3.0, ((0, 16),)),
        "outer_weight": noise_with(splits[5], (FF, D), FF ** -0.5, 0.0546875, ((0, 16),), (0, 1, 16, 2.0)),
        "outer_bias": noise(splits[6], (D,), 0.5, 3.0, ((0, 8),)),
    }


epsilon = 1e-06

def reference(tokens, row_image, norm_gain, inner_weight, inner_bias, outer_weight, outer_bias):
    values = tokens.astype(jnp.float32)
    row_mean = lax.optimization_barrier(jnp.mean(values, axis=1, keepdims=True))
    row_var = lax.optimization_barrier(jnp.mean(values * values, axis=1, keepdims=True)) - row_mean * row_mean
    normed = ((values - row_mean) * lax.rsqrt(row_var + epsilon) * norm_gain.astype(jnp.float32)).astype(jnp.bfloat16)
    pre_act = jnp.dot(normed, inner_weight, preferred_element_type=jnp.float32) + inner_bias.astype(jnp.float32)
    hidden = jax.nn.gelu(pre_act, approximate=False).astype(jnp.bfloat16)
    branch_out = jnp.dot(hidden, outer_weight, preferred_element_type=jnp.float32)
    live_rows = (row_image < IMAGES)[:, None]
    summed = values + branch_out + outer_bias.astype(jnp.float32)
    mixed_rows = jnp.where(live_rows, summed, jnp.zeros_like(summed)).astype(jnp.bfloat16)
    member = row_image[None, :] == jnp.arange(IMAGES, dtype=jnp.int32)[:, None]
    pooled_sums = jnp.dot(member.astype(jnp.bfloat16), mixed_rows, preferred_element_type=jnp.float32)
    image_counts = lax.optimization_barrier(jnp.sum(member.astype(jnp.float32), axis=1, keepdims=True))
    return (mixed_rows, pooled_sums / image_counts)
```

```python
import jax
import jax.numpy as jnp
from jax import lax
from jax.sharding import PartitionSpec as P

SEND = 32
KEEP = 160
IMAGES = 10
EPSILON = 1e-06
PAIR = [(0, 1), (1, 0)]


def swap_dp(array):
    return lax.ppermute(array, "dp", PAIR)


def finish(row_image, offset, work_values, branch_out, outer_bias):
    rows, cols = row_image.shape[0], work_values.shape[1]
    result_rows = (work_values + branch_out + outer_bias.astype(jnp.float32)).astype(jnp.bfloat16)
    returned = swap_dp(result_rows[KEEP - SEND :])
    row_ids = jnp.arange(rows, dtype=jnp.int32)[:, None]
    placed = lax.dynamic_update_slice_in_dim(
        jnp.zeros((rows, cols), jnp.bfloat16), result_rows, offset, 0
    )
    returned_pad = jnp.concatenate(
        [returned, jnp.zeros((rows - SEND, cols), jnp.bfloat16)], axis=0
    )
    mixed_rows = jnp.where(row_ids < offset, returned_pad, placed)
    live_rows = (row_image < IMAGES)[:, None]
    mixed_rows = jnp.where(live_rows, mixed_rows, jnp.zeros_like(mixed_rows))
    member = row_image[None, :] == jnp.arange(IMAGES, dtype=jnp.int32)[:, None]
    pooled_sums = jnp.dot(
        member.astype(jnp.bfloat16), mixed_rows, preferred_element_type=jnp.float32
    )
    image_counts = jnp.sum(member.astype(jnp.float32), axis=1)
    pooled_sums, image_counts = lax.psum((pooled_sums, image_counts), "dp")
    return mixed_rows, pooled_sums / image_counts[:, None]


def general(tokens, row_image, norm_gain, inner_weight, inner_bias, outer_weight, outer_bias):
    width = inner_weight.shape[0] * lax.axis_size("dp") * lax.axis_size("mp")
    offset = jnp.where(row_image[KEEP] < IMAGES, SEND, 0).astype(jnp.int32)
    incoming = swap_dp(tokens[:SEND])
    own_rows = lax.dynamic_slice_in_dim(tokens, offset, KEEP - SEND, 0)
    tail_rows = jnp.where(offset > 0, tokens[KEEP:], incoming)
    work_values = jnp.concatenate([own_rows, tail_rows], axis=0).astype(jnp.float32)
    moments = lax.psum(
        (jnp.sum(work_values, axis=1), jnp.sum(work_values * work_values, axis=1)), "mp"
    )
    row_mean = (moments[0] / width)[:, None]
    row_var = (moments[1] / width)[:, None] - row_mean * row_mean
    own_normed = (
        (work_values - row_mean) * lax.rsqrt(row_var + EPSILON) * norm_gain.astype(jnp.float32)
    ).astype(jnp.bfloat16)
    normed = lax.all_gather(own_normed, "mp", axis=1, tiled=True)
    normed = lax.all_gather(normed, "dp", axis=0, tiled=True)
    slab = lax.axis_index("dp") * lax.axis_size("mp") + lax.axis_index("mp")
    features = inner_weight.shape[0]
    normed = lax.dynamic_slice_in_dim(normed, slab * features, features, 1)
    pre_act = jnp.dot(normed, inner_weight, preferred_element_type=jnp.float32)
    pre_act = lax.psum_scatter(pre_act, "dp", scatter_dimension=1, tiled=True)
    pre_act = lax.psum_scatter(pre_act, "mp", scatter_dimension=1, tiled=True)
    hidden = jax.nn.gelu(pre_act + inner_bias.astype(jnp.float32), approximate=False).astype(
        jnp.bfloat16
    )
    branch_out = jnp.dot(hidden, outer_weight, preferred_element_type=jnp.float32)
    branch_out = lax.psum_scatter(branch_out, "dp", scatter_dimension=0, tiled=True)
    branch_out = lax.psum_scatter(branch_out, "mp", scatter_dimension=1, tiled=True)
    return finish(row_image, offset, work_values, branch_out, outer_bias)


def solution(mesh):
    return jax.shard_map(
        general,
        mesh=mesh,
        in_specs=(
            P(("groups", "dp"), "mp"),
            P(("groups", "dp")),
            P("mp"),
            P(("dp", "mp"), None),
            P(("dp", "mp")),
            P(("dp", "mp"), None),
            P("mp"),
        ),
        out_specs=(P(("groups", "dp"), "mp"), P("groups", "mp")),
        check_vma=False,
    )
```

```python
import jax
import jax.numpy as jnp
from jax import lax
from jax.sharding import PartitionSpec as P

SEND = 32
KEEP = 160
IMAGES = 10
EPSILON = 1e-06
PARTS = 1
PAIR = [(0, 1), (1, 0)]


def swap_dp(array):
    return lax.ppermute(array, "dp", PAIR)


def finish(row_image, offset, work_values, branch_out, outer_bias):
    rows, cols = row_image.shape[0], work_values.shape[1]
    result_rows = (work_values + branch_out + outer_bias.astype(jnp.float32)).astype(jnp.bfloat16)
    returned = swap_dp(result_rows[KEEP - SEND :])
    row_ids = jnp.arange(rows, dtype=jnp.int32)[:, None]
    placed = lax.dynamic_update_slice_in_dim(
        jnp.zeros((rows, cols), jnp.bfloat16), result_rows, offset, 0
    )
    returned_pad = jnp.concatenate(
        [returned, jnp.zeros((rows - SEND, cols), jnp.bfloat16)], axis=0
    )
    mixed_rows = jnp.where(row_ids < offset, returned_pad, placed)
    live_rows = (row_image < IMAGES)[:, None]
    mixed_rows = jnp.where(live_rows, mixed_rows, jnp.zeros_like(mixed_rows))
    member = row_image[None, :] == jnp.arange(IMAGES, dtype=jnp.int32)[:, None]
    pooled_sums = jnp.dot(
        member.astype(jnp.bfloat16), mixed_rows, preferred_element_type=jnp.float32
    )
    image_counts = jnp.sum(member.astype(jnp.float32), axis=1)
    pooled_sums, image_counts = lax.psum((pooled_sums, image_counts), "dp")
    return mixed_rows, pooled_sums / image_counts[:, None]


def general(tokens, row_image, norm_gain, inner_weight, inner_bias, outer_weight, outer_bias):
    width = inner_weight.shape[0] * lax.axis_size("dp") * lax.axis_size("mp")
    offset = jnp.where(row_image[KEEP] < IMAGES, SEND, 0).astype(jnp.int32)
    incoming = swap_dp(tokens[:SEND])
    own_rows = lax.dynamic_slice_in_dim(tokens, offset, KEEP - SEND, 0)
    tail_rows = jnp.where(offset > 0, tokens[KEEP:], incoming)
    work_values = jnp.concatenate([own_rows, tail_rows], axis=0).astype(jnp.float32)
    moments = lax.psum(
        (jnp.sum(work_values, axis=1), jnp.sum(work_values * work_values, axis=1)), "mp"
    )
    row_mean = (moments[0] / width)[:, None]
    row_var = (moments[1] / width)[:, None] - row_mean * row_mean
    own_normed = (
        (work_values - row_mean) * lax.rsqrt(row_var + EPSILON) * norm_gain.astype(jnp.float32)
    ).astype(jnp.bfloat16)
    normed = lax.all_gather(own_normed, "mp", axis=1, tiled=True)
    normed = lax.all_gather(normed, "dp", axis=0, tiled=True)
    slab = lax.axis_index("dp") * lax.axis_size("mp") + lax.axis_index("mp")
    features = inner_weight.shape[0]
    normed = lax.dynamic_slice_in_dim(normed, slab * features, features, 1)
    pre_act = jnp.dot(normed, inner_weight, preferred_element_type=jnp.float32)
    pre_act = lax.psum_scatter(pre_act, "dp", scatter_dimension=1, tiled=True)
    pre_act = lax.psum_scatter(pre_act, "mp", scatter_dimension=1, tiled=True)
    hidden = jax.nn.gelu(pre_act + inner_bias.astype(jnp.float32), approximate=False).astype(
        jnp.bfloat16
    )
    branch_out = jnp.dot(hidden, outer_weight, preferred_element_type=jnp.float32)
    branch_out = lax.psum_scatter(branch_out, "dp", scatter_dimension=0, tiled=True)
    branch_out = lax.psum_scatter(branch_out, "mp", scatter_dimension=1, tiled=True)
    return finish(row_image, offset, work_values, branch_out, outer_bias)


ACROSS = [(i, i ^ 1) for i in range(8)]
ORDER = ((3, 2, 1, 0), (3, 2, 0, 1), (0, 1, 3, 2), (0, 1, 2, 3))
DEPTH = 2


def along_z(*moves):
    return [(2 * a + x, 2 * b + x) for a, b in moves for x in (0, 1)]


ENDS_IN = along_z((0, 1), (3, 2))
UP_TWO = along_z((0, 1), (1, 2))
DOWN_TWO = along_z((3, 2), (2, 1))
UP_ALL = along_z((0, 1), (1, 2), (2, 3))
DOWN_ALL = along_z((3, 2), (2, 1), (1, 0))


def shift(array, moves):
    return lax.ppermute(array.astype(jnp.bfloat16), "mp", moves).astype(jnp.float32)


def after(array, other):
    return lax.optimization_barrier((array, other))[0]


class Across:
    def __init__(self):
        self.done = []

    def send(self, array):
        array = array.astype(jnp.bfloat16)
        if len(self.done) >= DEPTH:
            array = after(array, self.done[-DEPTH])
        self.done.append(lax.ppermute(array, "mp", ACROSS))
        return self.done[-1].astype(jnp.float32)


class Scatter:
    def __init__(self, across, block, z):
        self.across, self.block, self.z = across, block, z
        self.kept = []

    def step(self):
        step, z, kept = len(self.kept), self.z, self.kept
        sent, own = self.block(step)
        kept.append(own + self.across.send(sent))
        if step == 0:
            self.first = shift(kept[0], ENDS_IN)
        elif step == 1:
            ends = (z == 0) | (z == 3)
            second = jnp.where(ends, kept[1], kept[0] + self.first).astype(jnp.bfloat16)
            self.up, self.down = shift(second, UP_TWO), shift(second, DOWN_TWO)
        elif step == 2:
            up = jnp.where(z == 1, kept[1], kept[2]) + self.up
            down = jnp.where(z == 2, kept[1], kept[2]) + self.down
            self.up, self.down = shift(up, UP_ALL), shift(down, DOWN_ALL)
        else:
            return kept[3] + self.up + self.down


def eight(tokens, row_image, norm_gain, inner_weight, inner_bias, outer_weight, outer_bias):
    shard_rows, cols = tokens.shape
    features, units = inner_weight.shape
    half = cols // 2
    width = cols * 8
    dp, mp = lax.axis_index("dp"), lax.axis_index("mp")
    x, z = lax.rem(mp, 2), mp // 2
    order = jnp.asarray(ORDER, jnp.int32)[z]
    loaded = row_image[KEEP] < IMAGES

    sheet = jnp.concatenate([tokens, jnp.broadcast_to(norm_gain[None, :], (16, cols))], axis=0)
    upper = mp // 4
    same = lax.dynamic_slice_in_dim(sheet, upper * half, half, 1)
    other = lax.dynamic_slice_in_dim(sheet, (1 - upper) * half, half, 1)
    same = lax.ppermute(same, "mp", [(4 * e + q, 2 * q + e) for e in (0, 1) for q in range(4)])
    other = lax.ppermute(other, "mp", [(4 * e + q, 2 * q + 1 - e) for e in (0, 1) for q in range(4)])

    values = tokens.astype(jnp.float32)
    moments = jnp.stack([jnp.sum(values, axis=1), jnp.sum(values * values, axis=1)])
    moments = moments + lax.ppermute(moments, "mp", [(i, i ^ 1) for i in range(8)])
    inner_weight = after(inner_weight, moments)
    for bit in (2, 4):
        moments = moments + lax.ppermute(moments, "mp", [(i, i ^ bit) for i in range(8)])
    row_mean = (moments[0] / width)[:, None]
    row_var = (moments[1] / width)[:, None] - row_mean * row_mean
    scale = lax.rsqrt(row_var + EPSILON)

    low_first = x == dp
    slab = jnp.where(
        low_first,
        jnp.concatenate([same, other], axis=1),
        jnp.concatenate([other, same], axis=1),
    ).astype(jnp.float32)
    own = ((slab[:shard_rows] - row_mean) * scale * slab[shard_rows : shard_rows + 1]).astype(
        jnp.bfloat16
    )
    theirs = swap_dp(own)
    theirs = jnp.concatenate([theirs[:, half:], theirs[:, :half]], axis=1)
    my_work = jnp.where(
        loaded, own[SEND:], jnp.concatenate([own[: KEEP - SEND], theirs[:SEND]], axis=0)
    )
    their_work = jnp.where(
        loaded, jnp.concatenate([theirs[: KEEP - SEND], own[:SEND]], axis=0), theirs[SEND:]
    )
    edges = [(i * KEEP // PARTS, (i + 1) * KEEP // PARTS) for i in range(PARTS)]
    parts = [
        lax.optimization_barrier(jnp.concatenate([my_work[a:b], their_work[a:b]], axis=0))
        for a, b in edges
    ]

    pair = units // 8
    one = pair // 2
    lent = []
    for step in range(4):
        start = (1 - dp) * (units // 2) + order[step] * pair
        lent.append(swap_dp(lax.dynamic_slice_in_dim(inner_weight, start, pair, 1)))

    def inner_block(rows):
        def block(step):
            def product(side):
                mine = lax.dynamic_slice_in_dim(
                    inner_weight, dp * (units // 2) + order[step] * pair + side * one, one, 1
                )
                got = lax.dynamic_slice_in_dim(lent[step], side * one, one, 1)
                return jnp.dot(
                    rows[:, :features], mine, preferred_element_type=jnp.float32
                ) + jnp.dot(rows[:, features:], got, preferred_element_type=jnp.float32)

            return product(1 - x), product(x)

        return block

    def outer_block(hidden):
        mine = hidden.shape[0] // 2

        def block(step):
            def product(side):
                start = order[step] * 2 * cols + side * cols
                weight = lax.dynamic_slice_in_dim(outer_weight, start, cols, 1)
                out = jnp.dot(hidden, weight, preferred_element_type=jnp.float32)
                return out[:mine] + swap_dp(out[mine:])

            return product(1 - x), product(x)

        return block

    def activate(pre_act):
        hidden = jax.nn.gelu(pre_act + inner_bias.astype(jnp.float32), approximate=False)
        return lax.optimization_barrier(hidden.astype(jnp.bfloat16))

    across = Across()
    inner = [Scatter(across, inner_block(rows), z) for rows in parts]
    outer, branch_out = [], []
    for i in range(PARTS):
        for step in range(4):
            pre_act = inner[i].step()
            if i and step > 1:
                branch_out.append(outer[-1].step())
                if step == 3:
                    branch_out.append(outer[-1].step())
            elif i and step == 1:
                outer[-1].step()
        outer.append(Scatter(across, outer_block(activate(pre_act)), z))
    for step in range(4):
        branch_out.append(outer[-1].step())
    branch_out = jnp.concatenate([part for part in branch_out if part is not None], axis=0)

    their_image = swap_dp(row_image)
    incoming = swap_dp(tokens[:SEND])
    work_tokens = jnp.where(
        loaded, tokens[SEND:], jnp.concatenate([tokens[: KEEP - SEND], incoming], axis=0)
    )
    work_image = jnp.where(
        loaded,
        row_image[SEND:],
        jnp.concatenate([row_image[: KEEP - SEND], their_image[:SEND]], axis=0),
    )
    result = (
        work_tokens.astype(jnp.float32) + branch_out + outer_bias.astype(jnp.float32)
    ).astype(jnp.bfloat16)
    result = jnp.where((work_image < IMAGES)[:, None], result, jnp.zeros_like(result))
    images = jnp.arange(IMAGES, dtype=jnp.int32)[:, None]
    sums = jnp.dot(
        (work_image[None, :] == images).astype(jnp.bfloat16),
        result,
        preferred_element_type=jnp.float32,
    )
    counts = jnp.sum((row_image[None, :] == images).astype(jnp.float32), axis=1) + jnp.sum(
        (their_image[None, :] == images).astype(jnp.float32), axis=1
    )
    returned = swap_dp(result[KEEP - SEND :])
    sums = sums + swap_dp(sums)
    mixed_rows = jnp.where(
        loaded,
        jnp.concatenate([returned, result], axis=0),
        jnp.concatenate(
            [result[: KEEP - SEND], jnp.zeros((shard_rows - KEEP + SEND, cols), jnp.bfloat16)], axis=0
        ),
    )
    return mixed_rows, sums / counts[:, None]


def solution(mesh):
    return jax.shard_map(
        eight if mesh.shape["mp"] == 8 and mesh.shape["dp"] == 2 else general,
        mesh=mesh,
        in_specs=(
            P(("groups", "dp"), "mp"),
            P(("groups", "dp")),
            P("mp"),
            P(("dp", "mp"), None),
            P(("dp", "mp")),
            P(("dp", "mp"), None),
            P("mp"),
        ),
        out_specs=(P(("groups", "dp"), "mp"), P("groups", "mp")),
        check_vma=False,
    )
```

```python
import jax
import jax.numpy as jnp
from jax import lax
from jax.experimental import pallas as pl
from jax.experimental.pallas import tpu as pltpu
from jax.sharding import PartitionSpec as P

SEND = 32
KEEP = 160
IMAGES = 10
EPSILON = 1e-06
PARTS = 1
PAIR = [(0, 1), (1, 0)]


def swap_dp(array):
    return lax.ppermute(array, "dp", PAIR)


def finish(row_image, offset, work_values, branch_out, outer_bias):
    rows, cols = row_image.shape[0], work_values.shape[1]
    result_rows = (work_values + branch_out + outer_bias.astype(jnp.float32)).astype(jnp.bfloat16)
    returned = swap_dp(result_rows[KEEP - SEND :])
    row_ids = jnp.arange(rows, dtype=jnp.int32)[:, None]
    placed = lax.dynamic_update_slice_in_dim(
        jnp.zeros((rows, cols), jnp.bfloat16), result_rows, offset, 0
    )
    returned_pad = jnp.concatenate(
        [returned, jnp.zeros((rows - SEND, cols), jnp.bfloat16)], axis=0
    )
    mixed_rows = jnp.where(row_ids < offset, returned_pad, placed)
    live_rows = (row_image < IMAGES)[:, None]
    mixed_rows = jnp.where(live_rows, mixed_rows, jnp.zeros_like(mixed_rows))
    member = row_image[None, :] == jnp.arange(IMAGES, dtype=jnp.int32)[:, None]
    pooled_sums = jnp.dot(
        member.astype(jnp.bfloat16), mixed_rows, preferred_element_type=jnp.float32
    )
    image_counts = jnp.sum(member.astype(jnp.float32), axis=1)
    pooled_sums, image_counts = lax.psum((pooled_sums, image_counts), "dp")
    return mixed_rows, pooled_sums / image_counts[:, None]


def general(tokens, row_image, norm_gain, inner_weight, inner_bias, outer_weight, outer_bias):
    width = inner_weight.shape[0] * lax.axis_size("dp") * lax.axis_size("mp")
    offset = jnp.where(row_image[KEEP] < IMAGES, SEND, 0).astype(jnp.int32)
    incoming = swap_dp(tokens[:SEND])
    own_rows = lax.dynamic_slice_in_dim(tokens, offset, KEEP - SEND, 0)
    tail_rows = jnp.where(offset > 0, tokens[KEEP:], incoming)
    work_values = jnp.concatenate([own_rows, tail_rows], axis=0).astype(jnp.float32)
    moments = lax.psum(
        (jnp.sum(work_values, axis=1), jnp.sum(work_values * work_values, axis=1)), "mp"
    )
    row_mean = (moments[0] / width)[:, None]
    row_var = (moments[1] / width)[:, None] - row_mean * row_mean
    own_normed = (
        (work_values - row_mean) * lax.rsqrt(row_var + EPSILON) * norm_gain.astype(jnp.float32)
    ).astype(jnp.bfloat16)
    normed = lax.all_gather(own_normed, "mp", axis=1, tiled=True)
    normed = lax.all_gather(normed, "dp", axis=0, tiled=True)
    slab = lax.axis_index("dp") * lax.axis_size("mp") + lax.axis_index("mp")
    features = inner_weight.shape[0]
    normed = lax.dynamic_slice_in_dim(normed, slab * features, features, 1)
    pre_act = jnp.dot(normed, inner_weight, preferred_element_type=jnp.float32)
    pre_act = lax.psum_scatter(pre_act, "dp", scatter_dimension=1, tiled=True)
    pre_act = lax.psum_scatter(pre_act, "mp", scatter_dimension=1, tiled=True)
    hidden = jax.nn.gelu(pre_act + inner_bias.astype(jnp.float32), approximate=False).astype(
        jnp.bfloat16
    )
    branch_out = jnp.dot(hidden, outer_weight, preferred_element_type=jnp.float32)
    branch_out = lax.psum_scatter(branch_out, "dp", scatter_dimension=0, tiled=True)
    branch_out = lax.psum_scatter(branch_out, "mp", scatter_dimension=1, tiled=True)
    return finish(row_image, offset, work_values, branch_out, outer_bias)


ACROSS = [(i, i ^ 1) for i in range(8)]
DIRECT_ORDER = tuple(tuple(z ^ (3 - i) for i in range(4)) for z in range(4))
ORDER = ((3, 2, 1, 0), (3, 2, 0, 1), (0, 1, 3, 2), (0, 1, 2, 3))
DEPTH = 2


def along_z(*moves):
    return [(2 * a + x, 2 * b + x) for a, b in moves for x in (0, 1)]


ENDS_IN = along_z((0, 1), (3, 2))
UP_TWO = along_z((0, 1), (1, 2))
DOWN_TWO = along_z((3, 2), (2, 1))
UP_ALL = along_z((0, 1), (1, 2), (2, 3))
DOWN_ALL = along_z((3, 2), (2, 1), (1, 0))


def shift(array, moves):
    return lax.ppermute(array.astype(jnp.bfloat16), "mp", moves).astype(jnp.float32)


def after(array, other):
    return lax.optimization_barrier((array, other))[0]


COST = pl.CostEstimate(flops=0, bytes_accessed=0, transcendentals=0)


def pieces(weight, starts, width, count):
    depth, each = weight.shape[0], starts.shape[0] // count

    def kernel(starts_ref, weight_ref, *rest):
        outs, (held, come, leave) = rest[:count], rest[count:]
        comes, leaves = [], []
        for i in range(count * each):
            begin = pl.multiple_of(starts_ref[i], 128)
            place = held.at[i // each, :, pl.ds(i % each * width, width)]
            comes.append(
                pltpu.make_async_copy(weight_ref.at[:, pl.ds(begin, width)], place, come.at[i])
            )
            comes[-1].start()
        for i in range(count):
            for copy in comes[i * each : (i + 1) * each]:
                copy.wait()
            leaves.append(pltpu.make_async_copy(held.at[i], outs[i], leave.at[i]))
            leaves[-1].start()
        for copy in leaves:
            copy.wait()

    shape = (depth, each * width)
    return pl.pallas_call(
        kernel,
        out_shape=[jax.ShapeDtypeStruct(shape, weight.dtype)] * count,
        in_specs=[
            pl.BlockSpec(memory_space=pltpu.SMEM),
            pl.BlockSpec(memory_space=pltpu.HBM),
        ],
        out_specs=[pl.BlockSpec(memory_space=pltpu.HBM)] * count,
        scratch_shapes=[
            pltpu.VMEM((count, *shape), weight.dtype),
            pltpu.SemaphoreType.DMA((count * each,)),
            pltpu.SemaphoreType.DMA((count,)),
        ],
        compiler_params=pltpu.CompilerParams(vmem_limit_bytes=40 << 20),
        cost_estimate=COST,
    )(starts, weight)


class Across:
    def __init__(self):
        self.done = []

    def send(self, array):
        array = array.astype(jnp.bfloat16)
        if len(self.done) >= DEPTH:
            array = after(array, self.done[-DEPTH])
        self.done.append(lax.ppermute(array, "mp", ACROSS))
        return self.done[-1].astype(jnp.float32)


class Scatter:
    def __init__(self, across, block, z, direct=False):
        self.across, self.block, self.z = across, block, z
        self.kept, self.direct = [], direct

    def step(self):
        step, z, kept = len(self.kept), self.z, self.kept
        sent, own = self.block(step)
        kept.append(own + self.across.send(sent))
        if self.direct:
            if step < 3:
                kept[-1] = shift(kept[-1], along_z(*((i, i ^ (3 - step)) for i in range(4))))
                return None
            return (kept[0] + kept[1]) + (kept[2] + kept[3])
        if step == 0:
            self.first = shift(kept[0], ENDS_IN)
        elif step == 1:
            ends = (z == 0) | (z == 3)
            second = jnp.where(ends, kept[1], kept[0] + self.first).astype(jnp.bfloat16)
            self.up, self.down = shift(second, UP_TWO), shift(second, DOWN_TWO)
        elif step == 2:
            up = jnp.where(z == 1, kept[1], kept[2]) + self.up
            down = jnp.where(z == 2, kept[1], kept[2]) + self.down
            self.up, self.down = shift(up, UP_ALL), shift(down, DOWN_ALL)
        else:
            return kept[3] + self.up + self.down


def eight(tokens, row_image, norm_gain, inner_weight, inner_bias, outer_weight, outer_bias):
    shard_rows, cols = tokens.shape
    features, units = inner_weight.shape
    half = cols // 2
    width = cols * 8
    dp, mp = lax.axis_index("dp"), lax.axis_index("mp")
    x, z = lax.rem(mp, 2), mp // 2
    order = jnp.asarray(ORDER, jnp.int32)[z]
    outer_order = jnp.asarray(DIRECT_ORDER, jnp.int32)[z]
    loaded = row_image[KEEP] < IMAGES

    sheet = jnp.concatenate([tokens, jnp.broadcast_to(norm_gain[None, :], (16, cols))], axis=0)
    upper = mp // 4
    same = lax.dynamic_slice_in_dim(sheet, upper * half, half, 1)
    other = lax.dynamic_slice_in_dim(sheet, (1 - upper) * half, half, 1)
    same = lax.ppermute(same, "mp", [(4 * e + q, 2 * q + e) for e in (0, 1) for q in range(4)])
    other = lax.ppermute(other, "mp", [(4 * e + q, 2 * q + 1 - e) for e in (0, 1) for q in range(4)])

    values = tokens.astype(jnp.float32)
    moments = jnp.stack([jnp.sum(values, axis=1), jnp.sum(values * values, axis=1)])
    moments = moments + lax.ppermute(moments, "mp", [(i, i ^ 1) for i in range(8)])
    moments, same, other = lax.optimization_barrier((moments, same, other))
    gate = moments
    moments = moments + sum(
        lax.ppermute(moments, "mp", [(i, i ^ bit) for i in range(8)]) for bit in (2, 4, 6)
    )
    row_mean = (moments[0] / width)[:, None]
    row_var = (moments[1] / width)[:, None] - row_mean * row_mean
    scale = lax.rsqrt(row_var + EPSILON)

    low_first = x == dp
    slab = jnp.where(
        low_first,
        jnp.concatenate([same, other], axis=1),
        jnp.concatenate([other, same], axis=1),
    ).astype(jnp.float32)
    own = ((slab[:shard_rows] - row_mean) * scale * slab[shard_rows : shard_rows + 1]).astype(
        jnp.bfloat16
    )
    theirs = swap_dp(own)
    theirs = jnp.concatenate([theirs[:, half:], theirs[:, :half]], axis=1)
    my_work = jnp.where(
        loaded, own[SEND:], jnp.concatenate([own[: KEEP - SEND], theirs[:SEND]], axis=0)
    )
    their_work = jnp.where(
        loaded, jnp.concatenate([theirs[: KEEP - SEND], own[:SEND]], axis=0), theirs[SEND:]
    )
    edges = [(i * KEEP // PARTS, (i + 1) * KEEP // PARTS) for i in range(PARTS)]
    parts = [
        lax.optimization_barrier(jnp.concatenate([my_work[a:b], their_work[a:b]], axis=0))
        for a, b in edges
    ]

    pair = units // 8
    one = pair // 2
    lent = []

    def lend(step, gate):
        start = after((1 - dp) * (units // 2) + order[step] * pair, gate)
        if step < 2:
            strip = pieces(inner_weight, start.reshape(1), pair, 1)[0]
        else:
            strip = lax.dynamic_slice_in_dim(inner_weight, start, pair, 1)
        lent.append(swap_dp(strip))

    lend(0, gate)

    def inner_block(rows):
        def block(step):
            def product(side):
                mine = lax.dynamic_slice_in_dim(
                    inner_weight, dp * (units // 2) + order[step] * pair + side * one, one, 1
                )
                got = lax.dynamic_slice_in_dim(lent[step], side * one, one, 1)
                return jnp.dot(
                    rows[:, :features], mine, preferred_element_type=jnp.float32
                ) + jnp.dot(rows[:, features:], got, preferred_element_type=jnp.float32)

            sent = product(1 - x)
            if step < 3:
                lend(step + 1, gate)
            return sent, product(x)

        return block

    def outer_block(hidden):
        mine = hidden.shape[0] // 2
        gates = []

        def block(step):
            given = hidden
            if step >= 2:
                given = after(hidden, gates[0])

            def product(side):
                start = outer_order[step] * 2 * cols + side * cols
                weight = lax.dynamic_slice_in_dim(outer_weight, start, cols, 1)
                out = jnp.dot(given, weight, preferred_element_type=jnp.float32)
                got = swap_dp(out[mine:])
                gates.append(got)
                return out[:mine] + got

            return product(1 - x), product(x)

        return block

    def activate(pre_act):
        hidden = jax.nn.gelu(pre_act + inner_bias.astype(jnp.float32), approximate=False)
        return lax.optimization_barrier(hidden.astype(jnp.bfloat16))

    across = Across()
    inner = [Scatter(across, inner_block(rows), z) for rows in parts]
    outer, branch_out = [], []
    for i in range(PARTS):
        for step in range(4):
            pre_act = inner[i].step()
            if i and step > 1:
                branch_out.append(outer[-1].step())
                if step == 3:
                    branch_out.append(outer[-1].step())
            elif i and step == 1:
                outer[-1].step()
        outer.append(Scatter(across, outer_block(activate(pre_act)), z, direct=True))
    for step in range(4):
        branch_out.append(outer[-1].step())
    branch_out = jnp.concatenate([part for part in branch_out if part is not None], axis=0)

    their_image = swap_dp(row_image)
    incoming = swap_dp(tokens[:SEND])
    work_tokens = jnp.where(
        loaded, tokens[SEND:], jnp.concatenate([tokens[: KEEP - SEND], incoming], axis=0)
    )
    work_image = jnp.where(
        loaded,
        row_image[SEND:],
        jnp.concatenate([row_image[: KEEP - SEND], their_image[:SEND]], axis=0),
    )
    result = (
        work_tokens.astype(jnp.float32) + branch_out + outer_bias.astype(jnp.float32)
    ).astype(jnp.bfloat16)
    result = jnp.where((work_image < IMAGES)[:, None], result, jnp.zeros_like(result))
    images = jnp.arange(IMAGES, dtype=jnp.int32)[:, None]
    sums = jnp.dot(
        (work_image[None, :] == images).astype(jnp.bfloat16),
        result,
        preferred_element_type=jnp.float32,
    )
    counts = jnp.sum((row_image[None, :] == images).astype(jnp.float32), axis=1) + jnp.sum(
        (their_image[None, :] == images).astype(jnp.float32), axis=1
    )
    returned = swap_dp(result[KEEP - SEND :])
    sums = sums + swap_dp(sums)
    mixed_rows = jnp.where(
        loaded,
        jnp.concatenate([returned, result], axis=0),
        jnp.concatenate(
            [result[: KEEP - SEND], jnp.zeros((shard_rows - KEEP + SEND, cols), jnp.bfloat16)], axis=0
        ),
    )
    return mixed_rows, sums / counts[:, None]


def solution(mesh):
    return jax.shard_map(
        eight if mesh.shape["mp"] == 8 and mesh.shape["dp"] == 2 else general,
        mesh=mesh,
        in_specs=(
            P(("groups", "dp"), "mp"),
            P(("groups", "dp")),
            P("mp"),
            P(("dp", "mp"), None),
            P(("dp", "mp")),
            P(("dp", "mp"), None),
            P("mp"),
        ),
        out_specs=(P(("groups", "dp"), "mp"), P("groups", "mp")),
        check_vma=False,
    )
```

```python
import jax
import jax.numpy as jnp
from jax import lax
from jax.experimental import pallas as pl
from jax.experimental.pallas import tpu as pltpu
from jax.sharding import PartitionSpec as P

SEND = 32
KEEP = 160
IMAGES = 10
EPSILON = 1e-06
PARTS = 1
PAIR = [(0, 1), (1, 0)]


def swap_dp(array):
    return lax.ppermute(array, "dp", PAIR)


def finish(row_image, offset, work_values, branch_out, outer_bias):
    rows, cols = row_image.shape[0], work_values.shape[1]
    result_rows = (work_values + branch_out + outer_bias.astype(jnp.float32)).astype(jnp.bfloat16)
    returned = swap_dp(result_rows[KEEP - SEND :])
    row_ids = jnp.arange(rows, dtype=jnp.int32)[:, None]
    placed = lax.dynamic_update_slice_in_dim(
        jnp.zeros((rows, cols), jnp.bfloat16), result_rows, offset, 0
    )
    returned_pad = jnp.concatenate(
        [returned, jnp.zeros((rows - SEND, cols), jnp.bfloat16)], axis=0
    )
    mixed_rows = jnp.where(row_ids < offset, returned_pad, placed)
    live_rows = (row_image < IMAGES)[:, None]
    mixed_rows = jnp.where(live_rows, mixed_rows, jnp.zeros_like(mixed_rows))
    member = row_image[None, :] == jnp.arange(IMAGES, dtype=jnp.int32)[:, None]
    pooled_sums = jnp.dot(
        member.astype(jnp.bfloat16), mixed_rows, preferred_element_type=jnp.float32
    )
    image_counts = jnp.sum(member.astype(jnp.float32), axis=1)
    pooled_sums, image_counts = lax.psum((pooled_sums, image_counts), "dp")
    return mixed_rows, pooled_sums / image_counts[:, None]


def general(tokens, row_image, norm_gain, inner_weight, inner_bias, outer_weight, outer_bias):
    width = inner_weight.shape[0] * lax.axis_size("dp") * lax.axis_size("mp")
    offset = jnp.where(row_image[KEEP] < IMAGES, SEND, 0).astype(jnp.int32)
    incoming = swap_dp(tokens[:SEND])
    own_rows = lax.dynamic_slice_in_dim(tokens, offset, KEEP - SEND, 0)
    tail_rows = jnp.where(offset > 0, tokens[KEEP:], incoming)
    work_values = jnp.concatenate([own_rows, tail_rows], axis=0).astype(jnp.float32)
    moments = lax.psum(
        (jnp.sum(work_values, axis=1), jnp.sum(work_values * work_values, axis=1)), "mp"
    )
    row_mean = (moments[0] / width)[:, None]
    row_var = (moments[1] / width)[:, None] - row_mean * row_mean
    own_normed = (
        (work_values - row_mean) * lax.rsqrt(row_var + EPSILON) * norm_gain.astype(jnp.float32)
    ).astype(jnp.bfloat16)
    normed = lax.all_gather(own_normed, "mp", axis=1, tiled=True)
    normed = lax.all_gather(normed, "dp", axis=0, tiled=True)
    slab = lax.axis_index("dp") * lax.axis_size("mp") + lax.axis_index("mp")
    features = inner_weight.shape[0]
    normed = lax.dynamic_slice_in_dim(normed, slab * features, features, 1)
    pre_act = jnp.dot(normed, inner_weight, preferred_element_type=jnp.float32)
    pre_act = lax.psum_scatter(pre_act, "dp", scatter_dimension=1, tiled=True)
    pre_act = lax.psum_scatter(pre_act, "mp", scatter_dimension=1, tiled=True)
    hidden = jax.nn.gelu(pre_act + inner_bias.astype(jnp.float32), approximate=False).astype(
        jnp.bfloat16
    )
    branch_out = jnp.dot(hidden, outer_weight, preferred_element_type=jnp.float32)
    branch_out = lax.psum_scatter(branch_out, "dp", scatter_dimension=0, tiled=True)
    branch_out = lax.psum_scatter(branch_out, "mp", scatter_dimension=1, tiled=True)
    return finish(row_image, offset, work_values, branch_out, outer_bias)


ACROSS = [(i, i ^ 1) for i in range(8)]
DIRECT_ORDER = tuple(tuple(z ^ (3 - i) for i in range(4)) for z in range(4))
ORDER = ((3, 2, 1, 0), (3, 2, 0, 1), (0, 1, 3, 2), (0, 1, 2, 3))
DEPTH = 3


def along_z(*moves):
    return [(2 * a + x, 2 * b + x) for a, b in moves for x in (0, 1)]


ENDS_IN = along_z((0, 1), (3, 2))
UP_TWO = along_z((0, 1), (1, 2))
DOWN_TWO = along_z((3, 2), (2, 1))
UP_ALL = along_z((0, 1), (1, 2), (2, 3))
DOWN_ALL = along_z((3, 2), (2, 1), (1, 0))


def shift(array, moves):
    return lax.ppermute(array.astype(jnp.bfloat16), "mp", moves).astype(jnp.float32)


def after(array, other):
    return lax.optimization_barrier((array, other))[0]


COST = pl.CostEstimate(flops=0, bytes_accessed=0, transcendentals=0)


def pieces(weight, starts, width, count):
    depth, each = weight.shape[0], starts.shape[0] // count

    def kernel(starts_ref, weight_ref, *rest):
        outs, (held, come, leave) = rest[:count], rest[count:]
        comes, leaves = [], []
        for i in range(count * each):
            begin = pl.multiple_of(starts_ref[i], 128)
            place = held.at[i // each, :, pl.ds(i % each * width, width)]
            comes.append(
                pltpu.make_async_copy(weight_ref.at[:, pl.ds(begin, width)], place, come.at[i])
            )
            comes[-1].start()
        for i in range(count):
            for copy in comes[i * each : (i + 1) * each]:
                copy.wait()
            leaves.append(pltpu.make_async_copy(held.at[i], outs[i], leave.at[i]))
            leaves[-1].start()
        for copy in leaves:
            copy.wait()

    shape = (depth, each * width)
    return pl.pallas_call(
        kernel,
        out_shape=[jax.ShapeDtypeStruct(shape, weight.dtype)] * count,
        in_specs=[
            pl.BlockSpec(memory_space=pltpu.SMEM),
            pl.BlockSpec(memory_space=pltpu.HBM),
        ],
        out_specs=[pl.BlockSpec(memory_space=pltpu.HBM)] * count,
        scratch_shapes=[
            pltpu.VMEM((count, *shape), weight.dtype),
            pltpu.SemaphoreType.DMA((count * each,)),
            pltpu.SemaphoreType.DMA((count,)),
        ],
        compiler_params=pltpu.CompilerParams(vmem_limit_bytes=40 << 20),
        cost_estimate=COST,
    )(starts, weight)


class Across:
    def __init__(self):
        self.done = []

    def send(self, array):
        array = array.astype(jnp.bfloat16)
        if len(self.done) >= DEPTH:
            array = after(array, self.done[-DEPTH])
        self.done.append(lax.ppermute(array, "mp", ACROSS))
        return self.done[-1].astype(jnp.float32)


class Scatter:
    def __init__(self, across, block, z, direct=False):
        self.across, self.block, self.z = across, block, z
        self.kept, self.direct = [], direct

    def step(self):
        step, z, kept = len(self.kept), self.z, self.kept
        sent, own = self.block(step)
        if step == 0 and not self.direct:
            cut = sent.shape[0] // 4
            parts = [own[:cut] + self.across.send(sent[:cut])]
            parts.append(own[cut:] + self.across.send(sent[cut:]))
            kept.append(jnp.concatenate(parts, axis=0))
            self.first = jnp.concatenate([shift(part, ENDS_IN) for part in parts], axis=0)
            return None
        kept.append(own + self.across.send(sent))
        if self.direct:
            if step < 3:
                kept[-1] = shift(kept[-1], along_z(*((i, i ^ (3 - step)) for i in range(4))))
                return None
            return (kept[0] + kept[1]) + (kept[2] + kept[3])
        if step == 0:
            self.first = shift(kept[0], ENDS_IN)
        elif step == 1:
            ends = (z == 0) | (z == 3)
            second = jnp.where(ends, kept[1], kept[0] + self.first).astype(jnp.bfloat16)
            self.up, self.down = shift(second, UP_TWO), shift(second, DOWN_TWO)
        elif step == 2:
            up = jnp.where(z == 1, kept[1], kept[2]) + self.up
            down = jnp.where(z == 2, kept[1], kept[2]) + self.down
            self.up, self.down = shift(up, UP_ALL), shift(down, DOWN_ALL)
        else:
            return kept[3] + self.up + self.down


def eight(tokens, row_image, norm_gain, inner_weight, inner_bias, outer_weight, outer_bias):
    shard_rows, cols = tokens.shape
    features, units = inner_weight.shape
    half = cols // 2
    width = cols * 8
    dp, mp = lax.axis_index("dp"), lax.axis_index("mp")
    x, z = lax.rem(mp, 2), mp // 2
    order = jnp.asarray(ORDER, jnp.int32)[z]
    outer_order = jnp.asarray(DIRECT_ORDER, jnp.int32)[z]
    loaded = row_image[KEEP] < IMAGES

    sheet = jnp.concatenate([tokens, jnp.broadcast_to(norm_gain[None, :], (16, cols))], axis=0)
    upper = mp // 4
    same = lax.dynamic_slice_in_dim(sheet, upper * half, half, 1)
    other = lax.dynamic_slice_in_dim(sheet, (1 - upper) * half, half, 1)
    same = lax.ppermute(same, "mp", [(4 * e + q, 2 * q + e) for e in (0, 1) for q in range(4)])
    other = lax.ppermute(other, "mp", [(4 * e + q, 2 * q + 1 - e) for e in (0, 1) for q in range(4)])

    values = tokens.astype(jnp.float32)
    moments = jnp.stack([jnp.sum(values, axis=1), jnp.sum(values * values, axis=1)])
    moments = moments + lax.ppermute(moments, "mp", [(i, i ^ 1) for i in range(8)])
    moments, same, other = lax.optimization_barrier((moments, same, other))
    gate = moments
    moments = moments + sum(
        lax.ppermute(moments, "mp", [(i, i ^ bit) for i in range(8)]) for bit in (2, 4, 6)
    )
    row_mean = (moments[0] / width)[:, None]
    row_var = (moments[1] / width)[:, None] - row_mean * row_mean
    scale = lax.rsqrt(row_var + EPSILON)

    low_first = x == dp
    slab = jnp.where(
        low_first,
        jnp.concatenate([same, other], axis=1),
        jnp.concatenate([other, same], axis=1),
    ).astype(jnp.float32)
    own = ((slab[:shard_rows] - row_mean) * scale * slab[shard_rows : shard_rows + 1]).astype(
        jnp.bfloat16
    )
    theirs = swap_dp(own)
    theirs = jnp.concatenate([theirs[:, half:], theirs[:, :half]], axis=1)
    my_work = jnp.where(
        loaded, own[SEND:], jnp.concatenate([own[: KEEP - SEND], theirs[:SEND]], axis=0)
    )
    their_work = jnp.where(
        loaded, jnp.concatenate([theirs[: KEEP - SEND], own[:SEND]], axis=0), theirs[SEND:]
    )
    edges = [(i * KEEP // PARTS, (i + 1) * KEEP // PARTS) for i in range(PARTS)]
    parts = [
        lax.optimization_barrier(jnp.concatenate([my_work[a:b], their_work[a:b]], axis=0))
        for a, b in edges
    ]

    pair = units // 8
    one = pair // 2
    lent = []

    def lend(step, gate):
        start = after((1 - dp) * (units // 2) + order[step] * pair, gate)
        if step < 2:
            strip = pieces(inner_weight, start.reshape(1), pair, 1)[0]
        else:
            strip = lax.dynamic_slice_in_dim(inner_weight, start, pair, 1)
        lent.append(swap_dp(strip))

    lend(0, gate)

    def inner_block(rows):
        def block(step):
            def product(side):
                mine = lax.dynamic_slice_in_dim(
                    inner_weight, dp * (units // 2) + order[step] * pair + side * one, one, 1
                )
                got = lax.dynamic_slice_in_dim(lent[step], side * one, one, 1)
                return jnp.dot(
                    rows[:, :features], mine, preferred_element_type=jnp.float32
                ) + jnp.dot(rows[:, features:], got, preferred_element_type=jnp.float32)

            sent = product(1 - x)
            if step < 3:
                lend(step + 1, gate)
            return sent, product(x)

        return block

    def outer_block(hidden):
        mine = hidden.shape[0] // 2
        gates = []

        def block(step):
            given = hidden
            if step >= 2:
                given = after(hidden, gates[0])

            def product(side):
                start = outer_order[step] * 2 * cols + side * cols
                weight = lax.dynamic_slice_in_dim(outer_weight, start, cols, 1)
                out = jnp.dot(given, weight, preferred_element_type=jnp.float32)
                got = swap_dp(out[mine:])
                gates.append(got)
                return out[:mine] + got

            return product(1 - x), product(x)

        return block

    def activate(pre_act):
        hidden = jax.nn.gelu(pre_act + inner_bias.astype(jnp.float32), approximate=False)
        return lax.optimization_barrier(hidden.astype(jnp.bfloat16))

    across = Across()
    inner = [Scatter(across, inner_block(rows), z) for rows in parts]
    outer, branch_out = [], []
    for i in range(PARTS):
        for step in range(4):
            pre_act = inner[i].step()
            if i and step > 1:
                branch_out.append(outer[-1].step())
                if step == 3:
                    branch_out.append(outer[-1].step())
            elif i and step == 1:
                outer[-1].step()
        outer.append(Scatter(across, outer_block(activate(pre_act)), z, direct=True))
    for step in range(4):
        branch_out.append(outer[-1].step())
    branch_out = jnp.concatenate([part for part in branch_out if part is not None], axis=0)

    their_image = swap_dp(row_image)
    incoming = swap_dp(tokens[:SEND])
    work_tokens = jnp.where(
        loaded, tokens[SEND:], jnp.concatenate([tokens[: KEEP - SEND], incoming], axis=0)
    )
    work_image = jnp.where(
        loaded,
        row_image[SEND:],
        jnp.concatenate([row_image[: KEEP - SEND], their_image[:SEND]], axis=0),
    )
    result = (
        work_tokens.astype(jnp.float32) + branch_out + outer_bias.astype(jnp.float32)
    ).astype(jnp.bfloat16)
    result = jnp.where((work_image < IMAGES)[:, None], result, jnp.zeros_like(result))
    images = jnp.arange(IMAGES, dtype=jnp.int32)[:, None]
    sums = jnp.dot(
        (work_image[None, :] == images).astype(jnp.bfloat16),
        result,
        preferred_element_type=jnp.float32,
    )
    counts = jnp.sum((row_image[None, :] == images).astype(jnp.float32), axis=1) + jnp.sum(
        (their_image[None, :] == images).astype(jnp.float32), axis=1
    )
    returned = swap_dp(result[KEEP - SEND :])
    sums = sums + swap_dp(sums)
    mixed_rows = jnp.where(
        loaded,
        jnp.concatenate([returned, result], axis=0),
        jnp.concatenate(
            [result[: KEEP - SEND], jnp.zeros((shard_rows - KEEP + SEND, cols), jnp.bfloat16)], axis=0
        ),
    )
    return mixed_rows, sums / counts[:, None]


def solution(mesh):
    return jax.shard_map(
        eight if mesh.shape["mp"] == 8 and mesh.shape["dp"] == 2 else general,
        mesh=mesh,
        in_specs=(
            P(("groups", "dp"), "mp"),
            P(("groups", "dp")),
            P("mp"),
            P(("dp", "mp"), None),
            P(("dp", "mp")),
            P(("dp", "mp"), None),
            P("mp"),
        ),
        out_specs=(P(("groups", "dp"), "mp"), P("groups", "mp")),
        check_vma=False,
    )
```
